32 devices in a mesh: batch: 16 (over z, y, x), head: 2 (over core).
Axes of the slice: x: 2, y: 2, z: 4, core: 2. Of those that a mesh axis runs over, the one named last changes fastest.
Arguments:
- tokens: bfloat16 [24576, 768], P('batch'), may hold values from -6 to 6
- lengths: int32 [16, 3], P('batch'), may hold values from 1 to 1024, 1536 in all within a row
- norm1_gain: float32 [768], replicated, may hold values from 0.1 to 1.9
- norm1_bias: float32 [768], replicated, may hold values from -4 to 4
- qkv_weight: bfloat16 [768, 3, 768], P(None, None, 'head'), may hold values from -0.21875 to 0.21875
- out_weight: bfloat16 [768, 768], P('head'), may hold values from -1.75 to 1.75
- norm2_gain: float32 [768], replicated, may hold values from 0.1 to 1.9
- norm2_bias: float32 [768], replicated, may hold values from -4 to 4
- up_weight: bfloat16 [768, 3072], P(None, 'head'), may hold values from -0.21875 to 0.21875
- down_weight: bfloat16 [3072, 768], P('head'), may hold values from -0.109375 to 0.109375
- cotangent: bfloat16 [24576, 768], P('batch'), may hold values from -6 to 6
Outputs:
- block_out: bfloat16 [24576, 768], P('batch')
- grad_tokens: float32 [24576, 768], P('batch')
- grad_norm1_gain: float32 [768], P('batch')
- grad_norm1_bias: float32 [768], P('batch')
- grad_qkv: float32 [768, 3, 768], P('batch', None, 'head')
- grad_out: float32 [768, 768], P('head', 'batch')
- grad_norm2_gain: float32 [768], P('batch')
- grad_norm2_bias: float32 [768], P('batch')
- grad_up: float32 [768, 3072], P('batch', 'head')
- grad_down: float32 [3072, 768], P('head', 'batch')
The draws below stay inside these ranges and needn't reach their ends.
Inputs may be any that keep to these rules, and one draw needn't show every extreme that they name: Each row lists the lengths of the 3 documents of one batch group in order; a row sums to 1536, and its longest is 1024.
All inputs are finite; a program needn't handle non-finite values.
Results may differ from the reference program's by a relative error of at most 0.012.
The reference program's roundings to bfloat16 on the way count: a program that leaves them out, or rounds other values in their place, can miss the bound.
Values sent between devices are 32-bit elements; how exact they have to be, the bound alone decides.
A program may use at most 192 MiB of HBM per device.

```python
import math
import jax
import jax.numpy as jnp
import numpy as np
from jax import lax

D = 768
HD = 64
FF = 3072
DOCS = 3
TOK_DEV = 1536
SEQ_MAX = 1024
TOKENS = 24576
N_BATCH = 16


def with_spikes(entries, stream_key, source, target, parts, factor):
    def block_of(position):
        return (jnp.arange(entries.shape[position]) // (entries.shape[position] // parts)).reshape((-1,) + (1,) * (entries.ndim - 1 - position))

    first = jax.random.permutation(stream_key, parts)[block_of(target)]
    far = (block_of(target) + parts // 2) % parts
    return jnp.where((block_of(source) == first) | (block_of(source) == far), factor * entries, entries)


def shard_levels(stream_key, extent, shards, least, largest):
    def one(dim, shards_of):
        steps = jax.random.uniform(jax.random.fold_in(jax.random.fold_in(stream_key, 6), dim), (shards_of,), jnp.float32, least / len(shards), largest / len(shards))
        return jnp.repeat(jnp.exp(steps), extent[dim] // shards_of).reshape((-1,) + (1,) * (len(extent) - dim - 1))

    factor_of = one(*shards[0])
    for cut in shards[1:]:
        factor_of = factor_of * one(*cut)
    return factor_of


def profile(count, total, most, lean):
    loads = [(1 << 20) // math.isqrt(grade ** lean) + 1 for grade in range(2, count + 1)]
    surplus, given = total - most - (count - 1), [1] * (count - 1)
    while surplus > 0:
        free = [i for i in range(count - 1) if given[i] < most]
        pool, budget = sum([loads[i] for i in free]), surplus
        for i in free:
            extra = min(most - given[i], max(1, budget * loads[i] // pool), surplus)
            given[i] = given[i] + extra
            surplus = surplus - extra
    return np.array([most] + given)


def ragged(stream_key, number_of, total, reach, lean):
    if number_of == 2:
        one = jax.random.randint(stream_key, (), max(1, total - reach), min(reach, total - 1) + 1)
        return jnp.stack([one, total - one])
    sizes = jnp.asarray(profile(number_of, total, reach, lean), jnp.int32)
    pairs = (number_of - 1) // 2
    source_of, receiver = sizes[1:1 + 2 * pairs:2], sizes[2:2 + 2 * pairs:2]
    margin = jnp.minimum(source_of - 1, reach - receiver)
    moved = jax.random.randint(jax.random.fold_in(stream_key, 1), (pairs,), 0, 1 << 20) % (margin + 1)
    sizes = sizes.at[1:1 + 2 * pairs:2].set(source_of - moved).at[2:2 + 2 * pairs:2].set(receiver + moved)
    return sizes[jax.random.permutation(jax.random.fold_in(stream_key, 2), number_of)]


def gaussian(stream_key, shape, width, reach, split=(), held_as=jnp.bfloat16):
    values = jax.random.normal(stream_key, shape, jnp.float32) * width
    if len(split) > 0:
        values = shard_levels(stream_key, shape, split, -0.22, 0.18) * values
    return jnp.clip(values, min=-reach, max=reach).astype(held_as)


def heavy_noise(rng, dims, width, reach, cuts, heavy, kind=jnp.bfloat16):
    result = width * jax.random.normal(rng, dims, jnp.float32)
    if cuts:
        result = result * shard_levels(rng, dims, cuts, -0.22, 0.18)
    return jnp.clip(with_spikes(result, jax.random.fold_in(rng, 3), *heavy), -reach, reach).astype(kind)


def setup_inputs(seed: int = 0) -> dict:
    streams_of = jax.random.split(jax.random.key(seed), 12)
    return {
        "tokens": gaussian(streams_of[0], (TOKENS, D), 1.0, 6.0, ((0, 16),)),
        "lengths": jax.vmap(lambda own: ragged(own, DOCS, TOK_DEV, SEQ_MAX, 2))(jax.random.split(streams_of[1], N_BATCH)).reshape((N_BATCH, DOCS)).astype(jnp.int32),
        "norm1_gain": jnp.clip(1.0 + 0.18 * jax.random.normal(streams_of[2], (D,), jnp.float32), 0.1, 1.9),
        "norm1_bias": gaussian(streams_of[3], (D,), 0.3, 4.0, (), jnp.float32),
        "qkv_weight": gaussian(streams_of[4], (D, 3, D), D ** -0.5, 0.21875, ((2, 2),)),
        "out_weight": gaussian(streams_of[5], (D, D), (D // 64) ** -0.5, 1.75, ((0, 2),)),
        "norm2_gain": jnp.clip(1.0 + 0.18 * jax.random.normal(streams_of[6], (D,), jnp.float32), 0.1, 1.9),
        "norm2_bias": gaussian(streams_of[7], (D,), 0.3, 4.0, (), jnp.float32),
        "up_weight": gaussian(streams_of[8], (D, FF), D ** -0.5, 0.21875, ((1, 2),)),
        "down_weight": gaussian(streams_of[9], (FF, D), FF ** -0.5, 0.109375, ((0, 2),)),
        "cotangent": heavy_noise(streams_of[10], (TOKENS, D), 1.0, 6.0, ((0, 16),), (0, 1, 16, 2.0)),
    }


@jax.custom_vjp
def low(v):
    return lax.optimization_barrier(v.astype(jnp.bfloat16)).astype(jnp.float32)

@jax.custom_vjp
def low_back(v):
    return v

def low_keep(v):
    return (low(v), None)

def low_pass(kept, grad):
    return (grad,)

def back_keep(v):
    return (v, None)

def back_low(kept, grad):
    return (low(grad),)
low.defvjp(low_keep, low_pass)
low_back.defvjp(back_keep, back_low)
eps_norm = 1e-05
highest = lax.Precision.HIGHEST

def layer_norm(values_in, norm_gain, norm_bias):
    row_mean = lax.optimization_barrier(jnp.mean(values_in, axis=-1, keepdims=True))
    centered = values_in - row_mean
    variance = lax.optimization_barrier(jnp.mean(centered * centered, axis=-1, keepdims=True))
    return centered * lax.rsqrt(variance + eps_norm) * norm_gain + norm_bias

def group_block(tokens_in, doc_lengths, gain_one, bias_one, qkv_full, out_full, gain_two, bias_two, up_full, down_full):
    tok_count = tokens_in.shape[0]
    head_count = qkv_full.shape[2] // HD
    score_scale = 1.0 / math.sqrt(HD)
    normed_one = low(layer_norm(tokens_in, gain_one, bias_one))
    projected = jnp.einsum('td,dcf->tcf', normed_one, qkv_full, precision=highest)
    projected = low_back(low(projected)).reshape(tok_count, 3, head_count, HD).transpose(1, 2, 0, 3)
    doc_ends = jnp.cumsum(doc_lengths)
    places = jnp.arange(tok_count, dtype=jnp.int32)
    segment = lax.optimization_barrier(jnp.sum((places[:, None] >= doc_ends[None, :]).astype(jnp.int32), axis=1))
    allowed = (segment[:, None] == segment[None, :]) & (places[None, :] <= places[:, None])
    scores = jnp.einsum('hqd,hkd->hqk', projected[0], projected[1], precision=highest) * score_scale
    scores = low_back(scores)
    smooth_abs = jnp.sqrt(scores * scores + 1.0)
    masked = jnp.where(allowed[None], smooth_abs, -1000000000.0)
    row_top = lax.optimization_barrier(jnp.max(masked, axis=-1, keepdims=True))
    exp_terms = jnp.exp(masked - row_top)
    softmax_w = exp_terms / lax.optimization_barrier(jnp.sum(exp_terms, axis=-1, keepdims=True))
    signed_weights = low(scores / smooth_abs * softmax_w)
    attended = jnp.einsum('hqk,hkd->qhd', signed_weights, projected[2], precision=highest)
    attended = low_back(low(attended.reshape(tok_count, head_count * HD)))
    residual = tokens_in + low_back(jnp.dot(attended, out_full, precision=highest))
    normed_two = low(layer_norm(residual, gain_two, bias_two))
    up_pre = low_back(jnp.dot(normed_two, up_full, precision=highest))
    hidden = low(jax.nn.gelu(up_pre, approximate=True))
    return residual + jnp.dot(hidden, down_full, precision=highest)

def reference(tokens, lengths, norm1_gain, norm1_bias, qkv_weight, out_weight, norm2_gain, norm2_bias, up_weight, down_weight, cotangent):
    params = tuple((member.astype(jnp.float32) for member in (norm1_gain, norm1_bias, qkv_weight, out_weight, norm2_gain, norm2_bias, up_weight, down_weight)))
    inputs = tokens.astype(jnp.float32).reshape(N_BATCH, TOK_DEV, D)

    def forward(group_inputs, *weights_all):

        def group_step(item_pair):
            return group_block(item_pair[0], item_pair[1], *weights_all)
        return lax.map(jax.checkpoint(group_step), (group_inputs, lengths))
    block_out, pull_back = jax.vjp(forward, inputs, *params)
    gradients = pull_back(cotangent.astype(jnp.float32).reshape(N_BATCH, TOK_DEV, D))
    return (block_out.reshape(TOKENS, D).astype(jnp.bfloat16), gradients[0].reshape(TOKENS, D), gradients[1], gradients[2], gradients[3], gradients[4], gradients[5], gradients[6], gradients[7], gradients[8])
```

```python
import math

import jax
import jax.numpy as jnp
from jax import lax
from jax.experimental import pallas as pl
from jax.experimental.pallas import tpu as pltpu
from jax.sharding import PartitionSpec as P

HD=64
LOG2E=math.log2(math.e); LN2=math.log(2.0)
NT=(((1,),(1,)),((),()))
TN=(((0,),(0,)),((),()))

def dot(a,b,dims=(((1,),(0,)),((),()))):
    return lax.dot_general(a,b,dims,preferred_element_type=jnp.float32)

def doc_start(i,e0,e1):
    return jnp.where(i>=e1,e1,jnp.where(i>=e0,e0,0))

def fwd_kernel(lens,q_ref,k_ref,v_ref,att_ref,low_ref,lse_ref,vT,*,BQ,BK):
    qb=pl.program_id(1)
    row0=qb*BQ
    e0=lens[0]; e1=e0+lens[1]
    nk=k_ref.shape[0]//BK
    @pl.when(qb==0)
    def _():
        for b in range(nk):
            vT[b]=v_ref[b*BK:(b+1)*BK,:].T
    lane=lax.broadcasted_iota(jnp.int32,(1,128),1)
    q=q_ref[...]*jnp.bfloat16(0.125)
    qm=[jnp.where(lane<64,q,jnp.bfloat16(0)),jnp.where(lane>=64,q,jnp.bfloat16(0))]
    i=row0+lax.broadcasted_iota(jnp.int32,(1,BQ),1)
    st=doc_start(i,e0,e1)
    lo=doc_start(row0,e0,e1)//BK
    hi=(row0+BQ)//BK
    def body(kb,carry):
        out=[]
        k=k_ref[pl.ds(pl.multiple_of(kb*BK,BK),BK),:]
        j=kb*BK+lax.broadcasted_iota(jnp.int32,(BK,1),0)
        ok=(j>=st)&(j<=i)
        for h in range(2):
            m,l,acc=carry[h]
            s=dot(k,qm[h],NT)
            t=s*s+1.0
            r=lax.rsqrt(t)
            a=jnp.where(ok,(t*r)*LOG2E,-1e30)
            mn=jnp.maximum(m,jnp.max(a,axis=0,keepdims=True))
            al=jnp.exp2(m-mn)
            p=jnp.exp2(a-mn)
            l=l*al+jnp.sum(p,axis=0,keepdims=True)
            w=((s*r)*p).astype(jnp.bfloat16)
            acc=acc*al+dot(vT[kb,h*64:(h+1)*64,:],w)
            out.append((mn,l,acc))
        return tuple(out)
    z=(jnp.full((1,BQ),-1e30,jnp.float32),jnp.zeros((1,BQ),jnp.float32),jnp.zeros((64,BQ),jnp.float32))
    res=lax.fori_loop(lo,hi,body,(z,z))
    att=jnp.concatenate([res[h][2]/res[h][1] for h in range(2)],axis=0).T
    att_ref[...]=att
    low_ref[...]=att.astype(jnp.bfloat16)
    for h in range(2):
        lse_ref[0,h:h+1,:]=res[h][0]+jnp.log2(res[h][1])

def attn_fwd(lens,qkv,BQ=256,BK=256):
    T=qkv.shape[0]; npair=qkv.shape[1]//384
    return pl.pallas_call(
        lambda *a: fwd_kernel(*a,BQ=BQ,BK=BK),
        grid_spec=pltpu.PrefetchScalarGridSpec(num_scalar_prefetch=1,grid=(npair,T//BQ),
            in_specs=[pl.BlockSpec((BQ,128),lambda p,b,l:(b,p)),
                      pl.BlockSpec((T,128),lambda p,b,l:(0,npair+p)),
                      pl.BlockSpec((T,128),lambda p,b,l:(0,2*npair+p))],
            out_specs=[pl.BlockSpec((BQ,128),lambda p,b,l:(b,p)),
                       pl.BlockSpec((BQ,128),lambda p,b,l:(b,p)),
                       pl.BlockSpec((1,2,BQ),lambda p,b,l:(p,0,b))],
            scratch_shapes=[pltpu.VMEM((T//BK,128,BK),jnp.bfloat16)]),
        out_shape=[jax.ShapeDtypeStruct((T,npair*128),jnp.float32),
                   jax.ShapeDtypeStruct((T,npair*128),jnp.bfloat16),
                   jax.ShapeDtypeStruct((npair,2,T),jnp.float32)],
        name="attn_fwd",
        compiler_params=pltpu.CompilerParams(vmem_limit_bytes=48*2**20),
    )(lens,qkv,qkv,qkv)

def bwd_kernel(lens,q_ref,k_ref,v_ref,da_ref,att_ref,lse_ref,dq_ref,dk_ref,dv_ref,kT,dk_s,dv_s,*,BQ,BK):
    qb=pl.program_id(1)
    row0=qb*BQ
    e0=lens[0]; e1=e0+lens[1]
    T=k_ref.shape[0]
    nk=T//BK
    @pl.when(qb==0)
    def _():
        for b in range(nk):
            kT[b]=k_ref[b*BK:(b+1)*BK,:].T
        dk_s[...]=jnp.zeros_like(dk_s)
        dv_s[...]=jnp.zeros_like(dv_s)
    lane=lax.broadcasted_iota(jnp.int32,(1,128),1)
    zb=jnp.bfloat16(0)
    q=q_ref[...]*jnp.bfloat16(0.125)
    da=da_ref[...]
    qm=[jnp.where(lane<64,q,zb),jnp.where(lane>=64,q,zb)]
    dm=[jnp.where(lane<64,da,zb),jnp.where(lane>=64,da,zb)]
    prodT=(da.astype(jnp.float32)*att_ref[...]).T
    delta=[jnp.sum(prodT[h*64:(h+1)*64],axis=0,keepdims=True) for h in range(2)]
    i=row0+lax.broadcasted_iota(jnp.int32,(1,BQ),1)
    st=doc_start(i,e0,e1)
    lo=doc_start(row0,e0,e1)//BK
    hi=(row0+BQ)//BK
    lse=[lse_ref[0,h:h+1,:] for h in range(2)]
    def body(kb,carry):
        ks=pl.ds(pl.multiple_of(kb*BK,BK),BK)
        k=k_ref[ks,:]
        v=v_ref[ks,:]
        j=kb*BK+lax.broadcasted_iota(jnp.int32,(BK,1),0)
        ok=(j>=st)&(j<=i)
        out=[]
        dv=None; dk=None
        for h in range(2):
            s=dot(k,qm[h],NT)
            dw=dot(v,dm[h],NT)
            t=s*s+1.0
            r=lax.rsqrt(t)
            p=jnp.exp2(jnp.where(ok,(t*r)*LOG2E-lse[h],-1e30))
            sg=s*r
            w=(sg*p).astype(jnp.bfloat16)
            curv=1.0-(r*r)*(1.0-r)
            ds=(p*(dw*curv-sg*delta[h])).astype(jnp.bfloat16)
            x=dot(w,dm[h]); y=dot(ds,qm[h])
            dv=x if dv is None else dv+x
            dk=y if dk is None else dk+y
            out.append(carry[h]+dot(kT[kb,h*64:(h+1)*64,:],ds))
        dv_s[ks,:]+=dv
        dk_s[ks,:]+=dk
        return tuple(out)
    z=jnp.zeros((64,BQ),jnp.float32)
    res=lax.fori_loop(lo,hi,body,(z,z))
    dq_ref[...]=(jnp.concatenate(res,axis=0).T*0.125).astype(jnp.bfloat16)
    @pl.when(qb==pl.num_programs(1)-1)
    def _():
        dk_ref[...]=dk_s[...].astype(jnp.bfloat16)
        dv_ref[...]=dv_s[...].astype(jnp.bfloat16)

def attn_bwd(lens,qkv,datt,att,lse,BQ=256,BK=256):
    T=qkv.shape[0]; npair=qkv.shape[1]//384
    full=lambda off: pl.BlockSpec((T,128),lambda p,b,l:(0,off*npair+p))
    blk=pl.BlockSpec((BQ,128),lambda p,b,l:(b,p))
    o=jax.ShapeDtypeStruct((T,npair*128),jnp.bfloat16)
    return pl.pallas_call(
        lambda *a: bwd_kernel(*a,BQ=BQ,BK=BK),
        grid_spec=pltpu.PrefetchScalarGridSpec(num_scalar_prefetch=1,grid=(npair,T//BQ),
            in_specs=[blk,full(1),full(2),blk,blk,pl.BlockSpec((1,2,BQ),lambda p,b,l:(p,0,b))],
            out_specs=[blk,full(0),full(0)],
            scratch_shapes=[pltpu.VMEM((T//BK,128,BK),jnp.bfloat16),pltpu.VMEM((T,128),jnp.float32),pltpu.VMEM((T,128),jnp.float32)]),
        out_shape=[o,o,o],
        name="attn_bwd",
        compiler_params=pltpu.CompilerParams(vmem_limit_bytes=48*2**20),
    )(lens,qkv,qkv,qkv,datt,att,lse)


EPS = 1e-05


def norm_parts(rows):
    mean = jnp.mean(rows, axis=-1, keepdims=True)
    centered = rows - mean
    var = jnp.mean(centered * centered, axis=-1, keepdims=True)
    inv = lax.rsqrt(var + EPS)
    return centered * inv, inv


def norm_back(grad, hat, inv, gain):
    gg = grad * gain
    m1 = jnp.mean(gg, axis=-1, keepdims=True)
    m2 = jnp.mean(gg * hat, axis=-1, keepdims=True)
    return inv * (gg - m1 - hat * m2)


def swap_head(rows):
    return lax.ppermute(rows, "head", [(0, 1), (1, 0)])


def bit_groups(bits, first):
    order = [first, 1 - first] if bits > 1 else [0]
    groups = [[b] for b in order]
    rest = list(range(2, bits))
    while rest:
        groups.append(rest[:2])
        rest = rest[2:]
    return groups


def digit_of(index, group):
    digit = 0
    for bit in group:
        digit = digit * 2 + lax.rem(index // (1 << bit), 2)
    return digit


def xor_mask(group, e):
    mask = 0
    for place, bit in enumerate(reversed(group)):
        if (e >> place) & 1:
            mask |= 1 << bit
    return mask


def scatter_sum(grad, first):
    n = grad.shape[0]
    bits = n.bit_length() - 1
    me = lax.axis_index("batch")
    groups = bit_groups(bits, first)
    flat = [b for g in groups for b in g]
    cur = grad.reshape((2,) * bits + grad.shape[1:])
    cur = cur.transpose([bits - 1 - b for b in flat] + [bits, bits + 1])
    cur = cur.reshape(n, *grad.shape[1:])
    for group in groups:
        radix = 1 << len(group)
        digit = digit_of(me, group)
        view = cur.reshape(radix, cur.shape[0] // radix, *grad.shape[1:])
        total = lax.dynamic_index_in_dim(view, digit, 0, keepdims=False)
        for e in range(1, radix):
            piece = lax.dynamic_index_in_dim(view, digit ^ e, 0, keepdims=False)
            mask = xor_mask(group, e)
            total = total + lax.ppermute(piece, "batch", [(i, i ^ mask) for i in range(n)])
        cur = total
    return cur[0]


def scatter_both(grad):
    n = lax.axis_size("batch")
    view = grad.reshape(n, grad.shape[0] // n, grad.shape[1])
    half = grad.shape[1] // 2
    return jnp.concatenate(
        [scatter_sum(view[:, :, :half], 0), scatter_sum(view[:, :, half:], 1)], axis=1
    )


def shards(
    tokens,
    lengths,
    norm1_gain,
    norm1_bias,
    qkv_weight,
    out_weight,
    norm2_gain,
    norm2_bias,
    up_weight,
    down_weight,
    cotangent,
):
    n = lax.axis_size("batch")
    tok, width = tokens.shape
    cols = qkv_weight.shape[2]
    lens = lengths[0]
    x = tokens.astype(jnp.float32)
    hat1, inv1 = norm_parts(x)
    normed1 = (hat1 * norm1_gain + norm1_bias).astype(jnp.bfloat16)
    w_qkv = qkv_weight.reshape(width, 3 * cols)
    qkv = dot(normed1, w_qkv).astype(jnp.bfloat16)
    attended, att_low, lse = attn_fwd(lens, qkv)
    part = dot(att_low, out_weight)
    resid = x + part + swap_head(part)
    hat2, inv2 = norm_parts(resid)
    normed2 = (hat2 * norm2_gain + norm2_bias).astype(jnp.bfloat16)
    up_pre = dot(normed2, up_weight)
    hidden = jax.nn.gelu(up_pre, approximate=True).astype(jnp.bfloat16)
    grad_down = dot(cotangent, hidden, TN)
    d_hidden = dot(cotangent, down_weight, NT)
    d_up = jax.vjp(lambda u: jax.nn.gelu(u, approximate=True), up_pre)[1](d_hidden)[0]
    d_up = d_up.astype(jnp.bfloat16)
    g_down = scatter_both(grad_down)
    part2 = dot(d_up, up_weight, NT)
    grad_up = dot(normed2, d_up, TN)
    g_up = scatter_both(grad_up)
    mlp = dot(hidden, down_weight)
    block_out = (resid + (mlp + swap_head(mlp))).astype(jnp.bfloat16)
    d_normed2 = part2 + swap_head(part2)
    d_resid = cotangent.astype(jnp.float32) + norm_back(d_normed2, hat2, inv2, norm2_gain)
    d_branch = d_resid.astype(jnp.bfloat16)
    d_att = dot(d_branch, out_weight, NT).astype(jnp.bfloat16)
    grad_out = dot(d_branch, att_low, TN)
    dq, dk, dv = attn_bwd(lens, qkv, d_att, attended, lse)
    d_qkv = jnp.concatenate([dq, dk, dv], axis=1)
    part1 = dot(d_qkv, w_qkv, NT)
    grad_qkv = dot(normed1, d_qkv, TN)
    g_mix = scatter_both(jnp.concatenate([grad_out, grad_qkv], axis=1))
    d_normed1 = part1 + swap_head(part1)
    grad_tokens = d_resid + norm_back(d_normed1, hat1, inv1, norm1_gain)
    vectors = jnp.stack(
        [
            jnp.sum(d_normed1 * hat1, axis=0),
            jnp.sum(d_normed1, axis=0),
            jnp.sum(d_normed2 * hat2, axis=0),
            jnp.sum(d_normed2, axis=0),
        ]
    )
    vectors = vectors.reshape(4, n, width // n).transpose(1, 0, 2)
    g_vec = lax.psum_scatter(vectors, "batch", scatter_dimension=0, tiled=True)[0]
    return (
        block_out,
        grad_tokens,
        g_vec[0],
        g_vec[1],
        g_mix[:, cols:].reshape(width // n, 3, cols),
        g_mix[:, :cols].T,
        g_vec[2],
        g_vec[3],
        g_up,
        g_down.T,
    )


def solution(mesh):
    placed = (
        P("batch", None),
        P("batch", None),
        P(),
        P(),
        P(None, None, "head"),
        P("head", None),
        P(),
        P(),
        P(None, "head"),
        P("head", None),
        P("batch", None),
    )
    return jax.shard_map(
        shards,
        mesh=mesh,
        in_specs=placed,
        out_specs=(
            P("batch", None),
            P("batch", None),
            P("batch"),
            P("batch"),
            P("batch", None, "head"),
            P("head", "batch"),
            P("batch"),
            P("batch"),
            P("batch", "head"),
            P("head", "batch"),
        ),
        check_vma=False,
    )
```

```python
import math

import jax
import jax.numpy as jnp
from jax import lax
from jax.experimental import pallas as pl
from jax.experimental.pallas import tpu as pltpu
from jax.sharding import PartitionSpec as P

HD=64
LOG2E=math.log2(math.e); LN2=math.log(2.0)
NT=(((1,),(1,)),((),()))
TN=(((0,),(0,)),((),()))

def dot(a,b,dims=(((1,),(0,)),((),()))):
    return lax.dot_general(a,b,dims,preferred_element_type=jnp.float32)

def doc_start(i,e0,e1):
    return jnp.where(i>=e1,e1,jnp.where(i>=e0,e0,0))

def fwd_kernel(lens,q_ref,k_ref,v_ref,att_ref,low_ref,lse_ref,vT,*,BQ,BK):
    qb=pl.program_id(1)
    row0=qb*BQ
    e0=lens[0]; e1=e0+lens[1]
    nk=k_ref.shape[0]//BK
    @pl.when(qb==0)
    def _():
        for b in range(nk):
            vT[b]=v_ref[b*BK:(b+1)*BK,:].T
    lane=lax.broadcasted_iota(jnp.int32,(1,128),1)
    q=q_ref[...]*jnp.bfloat16(0.125)
    qm=[jnp.where(lane<64,q,jnp.bfloat16(0)),jnp.where(lane>=64,q,jnp.bfloat16(0))]
    i=row0+lax.broadcasted_iota(jnp.int32,(1,BQ),1)
    st=doc_start(i,e0,e1)
    lo=doc_start(row0,e0,e1)//BK
    hi=(row0+BQ)//BK
    def body(kb,carry):
        out=[]
        k=k_ref[pl.ds(pl.multiple_of(kb*BK,BK),BK),:]
        j=kb*BK+lax.broadcasted_iota(jnp.int32,(BK,1),0)
        ok=(j>=st)&(j<=i)
        for h in range(2):
            m,l,acc=carry[h]
            s=dot(k,qm[h],NT)
            t=s*s+1.0
            r=lax.rsqrt(t)
            a=jnp.where(ok,(t*r)*LOG2E,-1e30)
            mn=jnp.maximum(m,jnp.max(a,axis=0,keepdims=True))
            al=jnp.exp2(m-mn)
            p=jnp.exp2(a-mn)
            l=l*al+jnp.sum(p,axis=0,keepdims=True)
            w=((s*r)*p).astype(jnp.bfloat16)
            acc=acc*al+dot(vT[kb,h*64:(h+1)*64,:],w)
            out.append((mn,l,acc))
        return tuple(out)
    z=(jnp.full((1,BQ),-1e30,jnp.float32),jnp.zeros((1,BQ),jnp.float32),jnp.zeros((64,BQ),jnp.float32))
    res=lax.fori_loop(lo,hi,body,(z,z))
    att=jnp.concatenate([res[h][2]/res[h][1] for h in range(2)],axis=0).T
    att_ref[...]=att
    low_ref[...]=att.astype(jnp.bfloat16)
    for h in range(2):
        lse_ref[0,h:h+1,:]=res[h][0]+jnp.log2(res[h][1])

def attn_fwd(lens,qkv,BQ=256,BK=256):
    T=qkv.shape[0]; npair=qkv.shape[1]//384
    return pl.pallas_call(
        lambda *a: fwd_kernel(*a,BQ=BQ,BK=BK),
        grid_spec=pltpu.PrefetchScalarGridSpec(num_scalar_prefetch=1,grid=(npair,T//BQ),
            in_specs=[pl.BlockSpec((BQ,128),lambda p,b,l:(b,p)),
                      pl.BlockSpec((T,128),lambda p,b,l:(0,npair+p)),
                      pl.BlockSpec((T,128),lambda p,b,l:(0,2*npair+p))],
            out_specs=[pl.BlockSpec((BQ,128),lambda p,b,l:(b,p)),
                       pl.BlockSpec((BQ,128),lambda p,b,l:(b,p)),
                       pl.BlockSpec((1,2,BQ),lambda p,b,l:(p,0,b))],
            scratch_shapes=[pltpu.VMEM((T//BK,128,BK),jnp.bfloat16)]),
        out_shape=[jax.ShapeDtypeStruct((T,npair*128),jnp.float32),
                   jax.ShapeDtypeStruct((T,npair*128),jnp.bfloat16),
                   jax.ShapeDtypeStruct((npair,2,T),jnp.float32)],
        name="attn_fwd",
        compiler_params=pltpu.CompilerParams(vmem_limit_bytes=48*2**20),
    )(lens,qkv,qkv,qkv)

def bwd_kernel(lens,q_ref,k_ref,v_ref,da_ref,att_ref,lse_ref,dq_ref,dk_ref,dv_ref,kT,dk_s,dv_s,*,BQ,BK):
    qb=pl.program_id(1)
    row0=qb*BQ
    e0=lens[0]; e1=e0+lens[1]
    T=k_ref.shape[0]
    nk=T//BK
    @pl.when(qb==0)
    def _():
        for b in range(nk):
            kT[b]=k_ref[b*BK:(b+1)*BK,:].T
        dk_s[...]=jnp.zeros_like(dk_s)
        dv_s[...]=jnp.zeros_like(dv_s)
    lane=lax.broadcasted_iota(jnp.int32,(1,128),1)
    zb=jnp.bfloat16(0)
    q=q_ref[...]*jnp.bfloat16(0.125)
    da=da_ref[...]
    qm=[jnp.where(lane<64,q,zb),jnp.where(lane>=64,q,zb)]
    dm=[jnp.where(lane<64,da,zb),jnp.where(lane>=64,da,zb)]
    prodT=(da.astype(jnp.float32)*att_ref[...]).T
    delta=[jnp.sum(prodT[h*64:(h+1)*64],axis=0,keepdims=True) for h in range(2)]
    i=row0+lax.broadcasted_iota(jnp.int32,(1,BQ),1)
    st=doc_start(i,e0,e1)
    lo=doc_start(row0,e0,e1)//BK
    hi=(row0+BQ)//BK
    lse=[lse_ref[0,h:h+1,:] for h in range(2)]
    def body(kb,carry):
        ks=pl.ds(pl.multiple_of(kb*BK,BK),BK)
        k=k_ref[ks,:]
        v=v_ref[ks,:]
        j=kb*BK+lax.broadcasted_iota(jnp.int32,(BK,1),0)
        ok=(j>=st)&(j<=i)
        out=[]
        dv=None; dk=None
        for h in range(2):
            s=dot(k,qm[h],NT)
            dw=dot(v,dm[h],NT)
            t=s*s+1.0
            r=lax.rsqrt(t)
            p=jnp.exp2(jnp.where(ok,(t*r)*LOG2E-lse[h],-1e30))
            sg=s*r
            w=(sg*p).astype(jnp.bfloat16)
            curv=1.0-(r*r)*(1.0-r)
            ds=(p*(dw*curv-sg*delta[h])).astype(jnp.bfloat16)
            x=dot(w,dm[h]); y=dot(ds,qm[h])
            dv=x if dv is None else dv+x
            dk=y if dk is None else dk+y
            out.append(carry[h]+dot(kT[kb,h*64:(h+1)*64,:],ds))
        dv_s[ks,:]+=dv
        dk_s[ks,:]+=dk
        return tuple(out)
    z=jnp.zeros((64,BQ),jnp.float32)
    res=lax.fori_loop(lo,hi,body,(z,z))
    dq_ref[...]=(jnp.concatenate(res,axis=0).T*0.125).astype(jnp.bfloat16)
    @pl.when(qb==pl.num_programs(1)-1)
    def _():
        dk_ref[...]=dk_s[...].astype(jnp.bfloat16)
        dv_ref[...]=dv_s[...].astype(jnp.bfloat16)

def attn_bwd(lens,qkv,datt,att,lse,BQ=256,BK=256):
    T=qkv.shape[0]; npair=qkv.shape[1]//384
    full=lambda off: pl.BlockSpec((T,128),lambda p,b,l:(0,off*npair+p))
    blk=pl.BlockSpec((BQ,128),lambda p,b,l:(b,p))
    o=jax.ShapeDtypeStruct((T,npair*128),jnp.bfloat16)
    return pl.pallas_call(
        lambda *a: bwd_kernel(*a,BQ=BQ,BK=BK),
        grid_spec=pltpu.PrefetchScalarGridSpec(num_scalar_prefetch=1,grid=(npair,T//BQ),
            in_specs=[blk,full(1),full(2),blk,blk,pl.BlockSpec((1,2,BQ),lambda p,b,l:(p,0,b))],
            out_specs=[blk,full(0),full(0)],
            scratch_shapes=[pltpu.VMEM((T//BK,128,BK),jnp.bfloat16),pltpu.VMEM((T,128),jnp.float32),pltpu.VMEM((T,128),jnp.float32)]),
        out_shape=[o,o,o],
        name="attn_bwd",
        compiler_params=pltpu.CompilerParams(vmem_limit_bytes=48*2**20),
    )(lens,qkv,qkv,qkv,datt,att,lse)


EPS = 1e-05
MESH = pl.DeviceIdType.MESH
MB = 2**20


def norm_parts(rows):
    mean = jnp.mean(rows, axis=-1, keepdims=True)
    centered = rows - mean
    var = jnp.mean(centered * centered, axis=-1, keepdims=True)
    inv = lax.rsqrt(var + EPS)
    return centered * inv, inv


def norm_back(grad, hat, inv, gain):
    gg = grad * gain
    m1 = jnp.mean(gg, axis=-1, keepdims=True)
    m2 = jnp.mean(gg * hat, axis=-1, keepdims=True)
    return inv * (gg - m1 - hat * m2)


def qkv_kernel(x_ref, g_ref, b_ref, w_ref, qkv_ref, nT_ref):
    hat, _ = norm_parts(x_ref[...].astype(jnp.float32))
    normed = (hat * g_ref[...] + b_ref[...]).astype(jnp.bfloat16)
    nT_ref[...] = normed.T
    qkv_ref[...] = dot(normed, w_ref[...]).astype(jnp.bfloat16)


def norm_qkv(tokens, gain, bias, w, rows=256):
    T, D = tokens.shape
    C = w.shape[1]
    whole = lambda a, b: pl.BlockSpec((a, b), lambda i: (0, 0))
    return pl.pallas_call(
        qkv_kernel,
        grid=(T // rows,),
        in_specs=[
            pl.BlockSpec((rows, D), lambda i: (i, 0)),
            whole(1, D),
            whole(1, D),
            whole(D, C),
        ],
        out_specs=[
            pl.BlockSpec((rows, C), lambda i: (i, 0)),
            pl.BlockSpec((D, rows), lambda i: (0, i)),
        ],
        out_shape=[
            jax.ShapeDtypeStruct((T, C), jnp.bfloat16),
            jax.ShapeDtypeStruct((D, T), jnp.bfloat16),
        ],
        name="norm_qkv",
        compiler_params=pltpu.CompilerParams(vmem_limit_bytes=32 * MB),
    )(tokens, gain[None], bias[None], w)


def split_place(index, bits, first):
    order = [first, 1 - first] + list(range(2, bits)) if bits > 1 else [0]
    place = 0
    for bit in order:
        place = place * 2 + ((index >> bit) & 1)
    return place


GELU_A = math.sqrt(2.0 / math.pi)
GELU_B = GELU_A * 0.044715


def mlp_kernel(
    low_ref, ow_ref, x_ref, gain_ref, bias_ref, uw_ref, dw_ref, dy_ref,
    block_ref, resid_ref, hid_ref, dup_ref, ga_ref, gb_ref,
    part, got, got2, nT, dyT, stage, send_sem, recv_sem, send2, recv2, out_sem,
    *, n, R, CB,
):
    T, D = x_ref.shape
    F = uw_ref.shape[1]
    steps = T // R
    bits = n.bit_length() - 1
    rows = D // n
    other = 1 - lax.axis_index("head")
    barrier = pltpu.get_barrier_semaphore()
    pl.semaphore_signal(barrier, inc=1, device_id={"head": other}, device_id_type=MESH)
    pl.semaphore_wait(barrier, 1)

    def swap(c, dst, ssem, rsem):
        return pltpu.make_async_remote_copy(
            src_ref=part.at[c], dst_ref=dst.at[c], send_sem=ssem.at[c], recv_sem=rsem.at[c],
            device_id={"head": other}, device_id_type=MESH,
        )

    def at(c):
        return pl.ds(pl.multiple_of(c * R, R), R)

    @pl.loop(0, steps)
    def _(c):
        part[c] = dot(low_ref[at(c), :], ow_ref[...])
        swap(c, got, send_sem, recv_sem).start()

    @pl.loop(0, steps)
    def _(c):
        dyT[:, at(c)] = dy_ref[at(c), :].T

    @pl.loop(0, steps)
    def _(c):
        swap(c, got, send_sem, recv_sem).wait()
        resid = x_ref[at(c), :].astype(jnp.float32) + (part[c] + got[c])
        resid_ref[at(c), :] = resid
        hat, _ = norm_parts(resid)
        normed = (hat * gain_ref[...] + bias_ref[...]).astype(jnp.bfloat16)
        nT[:, at(c)] = normed.T
        for j in range(F // CB):
            js = slice(j * CB, (j + 1) * CB)
            u = dot(normed, uw_ref[:, js])
            d = dot(dy_ref[at(c), :], dw_ref[js, :], NT)
            u2 = u * u
            th = jnp.tanh(u * (GELU_A + GELU_B * u2))
            h = 0.5 + 0.5 * th
            hid_ref[at(c), js] = (u * h).astype(jnp.bfloat16)
            slope = h + (0.5 * u) * (1.0 - th * th) * (GELU_A + (3.0 * GELU_B) * u2)
            dup_ref[at(c), js] = (d * slope).astype(jnp.bfloat16)
        part[c] = dot(hid_ref[at(c), :], dw_ref[...])
        swap(c, got2, send2, recv2).start()

    def weight_grad(left, right_ref, out_ref, col0, base, first):
        width = stage.shape[-1]
        for j in range(F // 2 // width):
            slot = j % 2
            copy = pltpu.make_async_copy(
                stage.at[slot],
                out_ref.at[:, :, pl.ds(base + j * width, width)],
                out_sem.at[slot],
            )
            if j >= 2:
                copy.wait()
            g = dot(left[...], right_ref[:, col0 + j * width : col0 + (j + 1) * width])
            for b in range(n):
                stage[slot, split_place(b, bits, first)] = g[b * rows : (b + 1) * rows, :]
            copy.start()
        for j in range(min(2, F // 2 // width)):
            pltpu.make_async_copy(
                stage.at[j], out_ref.at[:, :, pl.ds(base + j * width, width)], out_sem.at[j]
            ).wait()

    weight_grad(dyT, hid_ref, ga_ref, 0, 0, 0)
    weight_grad(dyT, hid_ref, gb_ref, F // 2, 0, 1)
    weight_grad(nT, dup_ref, ga_ref, 0, F // 2, 0)
    weight_grad(nT, dup_ref, gb_ref, F // 2, F // 2, 1)

    @pl.loop(0, steps)
    def _(c):
        swap(c, got2, send2, recv2).wait()
        block_ref[at(c), :] = (resid_ref[at(c), :] + (part[c] + got2[c])).astype(jnp.bfloat16)


def mlp_block(low, out_w, x, gain, bias, up_w, down_w, dy, n, R=256, CB=512):
    T, D = x.shape
    F = up_w.shape[1]
    vm = pl.BlockSpec(memory_space=pltpu.VMEM)
    anyspec = pl.BlockSpec(memory_space=pl.ANY)
    sd = jax.ShapeDtypeStruct
    steps = T // R
    return pl.pallas_call(
        lambda *refs: mlp_kernel(*refs, n=n, R=R, CB=CB),
        in_specs=[vm] * 8,
        out_specs=[vm] * 4 + [anyspec] * 2,
        out_shape=[
            sd((T, D), jnp.bfloat16),
            sd((T, D), jnp.float32),
            sd((T, F), jnp.bfloat16),
            sd((T, F), jnp.bfloat16),
            sd((n, D // n, F), jnp.float32),
            sd((n, D // n, F), jnp.float32),
        ],
        scratch_shapes=[
            pltpu.VMEM((steps, R, D), jnp.float32),
            pltpu.VMEM((steps, R, D), jnp.float32),
            pltpu.VMEM((steps, R, D), jnp.float32),
            pltpu.VMEM((D, T), jnp.bfloat16),
            pltpu.VMEM((D, T), jnp.bfloat16),
            pltpu.VMEM((2, n, D // n, 256), jnp.float32),
            pltpu.SemaphoreType.DMA((steps,)),
            pltpu.SemaphoreType.DMA((steps,)),
            pltpu.SemaphoreType.DMA((steps,)),
            pltpu.SemaphoreType.DMA((steps,)),
            pltpu.SemaphoreType.DMA((2,)),
        ],
        name="mlp_block",
        compiler_params=pltpu.CompilerParams(
            collective_id=1, has_side_effects=True, vmem_limit_bytes=60 * MB
        ),
    )(low, out_w, x, gain[None], bias[None], up_w, down_w, dy)


def swap_head(rows):
    return lax.ppermute(rows, "head", [(0, 1), (1, 0)])


def bit_groups(bits, first):
    order = [first, 1 - first] if bits > 1 else [0]
    groups = [[b] for b in order]
    rest = list(range(2, bits))
    while rest:
        groups.append(rest[:2])
        rest = rest[2:]
    return groups


def digit_of(index, group):
    digit = 0
    for bit in group:
        digit = digit * 2 + lax.rem(index // (1 << bit), 2)
    return digit


def xor_mask(group, e):
    mask = 0
    for place, bit in enumerate(reversed(group)):
        if (e >> place) & 1:
            mask |= 1 << bit
    return mask


def scatter_sum(cur, first):
    n = cur.shape[0]
    me = lax.axis_index("batch")
    for group in bit_groups(n.bit_length() - 1, first):
        radix = 1 << len(group)
        digit = digit_of(me, group)
        view = cur.reshape(radix, cur.shape[0] // radix, *cur.shape[1:])
        total = lax.dynamic_index_in_dim(view, digit, 0, keepdims=False)
        for e in range(1, radix):
            piece = lax.dynamic_index_in_dim(view, digit ^ e, 0, keepdims=False)
            mask = xor_mask(group, e)
            total = total + lax.ppermute(piece, "batch", [(i, i ^ mask) for i in range(n)])
        cur = total
    return cur[0]


def scatter_both(grad):
    n = lax.axis_size("batch")
    bits = n.bit_length() - 1
    view = grad.reshape(n, grad.shape[0] // n, grad.shape[1])
    half = grad.shape[1] // 2
    parts = []
    for first in (0, 1):
        cut = view[:, :, first * half : (first + 1) * half]
        where = sorted(range(n), key=lambda b: split_place(b, bits, first))
        parts.append(scatter_sum(jnp.stack([cut[b] for b in where]), first))
    return jnp.concatenate(parts, axis=1)


def shards(
    tokens,
    lengths,
    norm1_gain,
    norm1_bias,
    qkv_weight,
    out_weight,
    norm2_gain,
    norm2_bias,
    up_weight,
    down_weight,
    cotangent,
):
    n = lax.axis_size("batch")
    tok, width = tokens.shape
    cols = qkv_weight.shape[2]
    half = up_weight.shape[1] // 2
    lens = lengths[0]
    w_qkv = qkv_weight.reshape(width, 3 * cols)
    qkv, normed1_t = norm_qkv(tokens, norm1_gain, norm1_bias, w_qkv)
    attended, att_low, lse = attn_fwd(lens, qkv)
    block_out, resid, hidden, d_up, grad_a, grad_b = mlp_block(
        att_low, out_weight, tokens, norm2_gain, norm2_bias, up_weight, down_weight, cotangent, n
    )
    got_a = scatter_sum(grad_a, 0)
    got_b = scatter_sum(grad_b, 1)
    hat2, inv2 = norm_parts(resid)
    part2 = dot(d_up, up_weight, NT)
    d_normed2 = part2 + swap_head(part2)
    d_resid = cotangent.astype(jnp.float32) + norm_back(d_normed2, hat2, inv2, norm2_gain)
    d_branch = d_resid.astype(jnp.bfloat16)
    d_att = dot(d_branch, out_weight, NT).astype(jnp.bfloat16)
    grad_out = dot(d_branch, att_low, TN)
    dq, dk, dv = attn_bwd(lens, qkv, d_att, attended, lse)
    d_qkv = jnp.concatenate([dq, dk, dv], axis=1)
    part1 = dot(d_qkv, w_qkv, NT)
    grad_qkv = dot(normed1_t, d_qkv)
    g_mix = scatter_both(jnp.concatenate([grad_out, grad_qkv], axis=1))
    d_normed1 = part1 + swap_head(part1)
    hat1, inv1 = norm_parts(tokens.astype(jnp.float32))
    grad_tokens = d_resid + norm_back(d_normed1, hat1, inv1, norm1_gain)
    vectors = jnp.stack(
        [
            jnp.sum(d_normed1 * hat1, axis=0),
            jnp.sum(d_normed1, axis=0),
            jnp.sum(d_normed2 * hat2, axis=0),
            jnp.sum(d_normed2, axis=0),
        ]
    )
    vectors = vectors.reshape(4, n, width // n).transpose(1, 0, 2)
    bits = n.bit_length() - 1
    where = sorted(range(n), key=lambda b: split_place(b, bits, 0))
    g_vec = scatter_sum(jnp.stack([vectors[b] for b in where]), 0)
    return (
        block_out,
        grad_tokens,
        g_vec[0],
        g_vec[1],
        g_mix[:, cols:].reshape(width // n, 3, cols),
        g_mix[:, :cols].T,
        g_vec[2],
        g_vec[3],
        jnp.concatenate([got_a[:, half:], got_b[:, half:]], axis=1),
        jnp.concatenate([got_a[:, :half], got_b[:, :half]], axis=1).T,
    )


def solution(mesh):
    placed = (
        P("batch", None),
        P("batch", None),
        P(),
        P(),
        P(None, None, "head"),
        P("head", None),
        P(),
        P(),
        P(None, "head"),
        P("head", None),
        P("batch", None),
    )
    return jax.shard_map(
        shards,
        mesh=mesh,
        in_specs=placed,
        out_specs=(
            P("batch", None),
            P("batch", None),
            P("batch"),
            P("batch"),
            P("batch", None, "head"),
            P("head", "batch"),
            P("batch"),
            P("batch"),
            P("batch", "head"),
            P("head", "batch"),
        ),
        check_vma=False,
    )
```
